512 devices in a mesh: dp: 64 (over y_hi, z, x), tensor: 8 (over y_lo, core).
Axes of the slice: x: 4, y: 8 (y_hi: 2, y_lo: 4; y = y_hi * 4 + y_lo), z: 8, core: 2. Of those that a mesh axis runs over, the one named last changes fastest.
Arguments:
- train_input: bfloat16 [16384, 5120], P('dp', 'tensor'), may hold values from -40 to 40
- train_preact: bfloat16 [16384, 20480], P('dp', 'tensor'), may hold values from -6 to 6
- train_upstream: bfloat16 [16384, 20480], P('dp', 'tensor'), may hold values from -6 to 6
- valid_input: bfloat16 [512, 5120], P('dp', 'tensor'), may hold values from -40 to 40
- valid_preact: bfloat16 [512, 20480], P('dp', 'tensor'), may hold values from -6 to 6
- valid_upstream: bfloat16 [512, 20480], P('dp', 'tensor'), may hold values from -6 to 6
Outputs:
- first_order: float32 [64, 2], P('dp')
- second_order: float32 [64], P('dp')
The draws below stay inside these ranges and needn't reach their ends.
All inputs are finite; a program needn't handle non-finite values.
Results may differ from the reference program's by a relative error of at most 0.0044.
Values may be sent and summed in bfloat16 or wider, within the bound.
No kernel may reach another device: no remote copies, remote signals or barrier semaphores. Data moves between devices by JAX's collectives and lax.ppermute only.
A program may use at most 64 MiB of HBM per device.

```python
import math
import jax
import jax.numpy as jnp
from jax import lax

D = 5120
FF = 20480
SEQ_LEN = 256
VAL_SEQS = 2
TRAIN_SEQS = 64
TRAIN_TOK = 16384
VAL_TOK = 512


def scaled_rows(key, base, rows, width):
    row_key, col_key = jax.random.split(key)
    row_scale = 10.0 ** jax.random.uniform(row_key, (rows, 1), jnp.float32, -0.5, 0.5)
    col_scale = 10.0 ** jax.random.uniform(col_key, (1, width), jnp.float32, -0.5, 0.5)
    return (base * row_scale * col_scale).astype(jnp.bfloat16)


def draw_train_input(key, part):
    key = jax.random.fold_in(key, 11)
    base_key = jax.random.fold_in(key, 0)
    scale_key = jax.random.fold_in(key, 2)
    base = jnp.clip(jax.random.normal(base_key, (TRAIN_TOK, D), jnp.float32), -4.0, 4.0)
    return scaled_rows(scale_key, base, TRAIN_TOK, D)


def draw_valid_input(key, part):
    key = jax.random.fold_in(key, 23)
    base_key = jax.random.fold_in(key, 0)
    scale_key = jax.random.fold_in(key, 2)
    base = jnp.clip(jax.random.normal(base_key, (VAL_TOK, D), jnp.float32), -4.0, 4.0)
    return scaled_rows(scale_key, base, VAL_TOK, D)


def steps_of(key, shape, cuts, low, high):
    loudness, own = 1.0, jax.random.fold_in(key, 6)
    for axis_at, blocks in cuts:
        steps = jnp.exp(jax.random.uniform(jax.random.fold_in(own, axis_at), (blocks,), jnp.float32, low / len(cuts), high / len(cuts)))
        loudness = loudness * jnp.repeat(steps, shape[axis_at] // blocks).reshape([-1 if axis == axis_at else 1 for axis in range(len(shape))])
    return loudness


def centred(rng, extent, deviation, bound, cuts=(), held_as=jnp.bfloat16):
    drawn = jax.random.normal(rng, extent, jnp.float32) * deviation
    if len(cuts) > 0:
        drawn = steps_of(rng, extent, cuts, -0.22, 0.18) * drawn
    return jnp.clip(drawn, min=-bound, max=bound).astype(held_as)


def setup_inputs(seed: int = 0) -> dict:
    arg_keys = jax.random.split(jax.random.key(seed), 7)
    train_input = draw_train_input(jax.random.fold_in(arg_keys[6], 71), 0)
    train_preact = centred(arg_keys[1], (TRAIN_TOK, FF), 1.0, 6.0, ((0, 64), (1, 8)))
    train_upstream = centred(arg_keys[2], (TRAIN_TOK, FF), 1.0, 6.0, ((0, 64), (1, 8)))
    valid_input = draw_valid_input(jax.random.fold_in(arg_keys[6], 71), 0)
    valid_preact = centred(arg_keys[4], (VAL_TOK, FF), 1.0, 6.0, ((0, 64), (1, 8)))
    valid_upstream = centred(arg_keys[5], (VAL_TOK, FF), 1.0, 6.0, ((0, 64), (1, 8)))
    return {"train_input": train_input, "train_preact": train_preact, "train_upstream": train_upstream, "valid_input": valid_input, "valid_preact": valid_preact, "valid_upstream": valid_upstream}


inv_root_two = 0.7071067811865476
inv_root_tau = 0.3989422804014327

def output_grad(preact, upstream):
    preact_f = preact.astype(jnp.float32)
    derivative = 0.5 * (1.0 + lax.erf(preact_f * inv_root_two)) + preact_f * jnp.exp(-0.5 * preact_f * preact_f) * inv_root_tau
    return (upstream.astype(jnp.float32) * derivative).astype(jnp.bfloat16)

def cross_dot(left, right):
    return lax.dot_general(left, right, (((1,), (1,)), ((), ())), preferred_element_type=jnp.float32)

def seq_scores(rows_input, rows_grad, valid_input, valid_grad):
    input_kernel = cross_dot(rows_input, valid_input) * (1.0 / math.sqrt(D))
    grad_kernel = cross_dot(rows_grad, valid_grad) * (1.0 / math.sqrt(FF))
    product = (input_kernel * grad_kernel).reshape(rows_input.shape[0], VAL_SEQS, SEQ_LEN)
    return lax.optimization_barrier(jnp.sum(product, axis=(0, 2))) * (1.0 / SEQ_LEN)

def reference(train_input, train_preact, train_upstream, valid_input, valid_preact, valid_upstream):
    valid_grad = output_grad(valid_preact, valid_upstream)

    def one_train(items):
        seq_input, seq_preact, seq_upstream = items
        seq_grad = output_grad(seq_preact, seq_upstream)
        return seq_scores(seq_input, seq_grad, valid_input, valid_grad)
    first_order = lax.map(one_train, (train_input.reshape(TRAIN_SEQS, SEQ_LEN, D), train_preact.reshape(TRAIN_SEQS, SEQ_LEN, FF), train_upstream.reshape(TRAIN_SEQS, SEQ_LEN, FF)))
    weight = lax.optimization_barrier(jnp.sum(first_order, axis=0))
    second_order = lax.optimization_barrier(jnp.sum(first_order * weight[None, :], axis=1))
    return (first_order, second_order)
```

```python
import math

import jax
import jax.numpy as jnp
from jax import lax
from jax.sharding import Mesh, PartitionSpec as P

D = 5120
FF = 20480
SEQ_LEN = 256
VAL_SEQS = 2
DP = ("yh", "z", "x")
TENSOR = ("yl", "core")
SIZES = (2, 8, 4, 4, 2)

inv_root_two = 0.7071067811865476
inv_root_tau = 0.3989422804014327


def output_grad(preact, upstream):
    preact_f = preact.astype(jnp.float32)
    derivative = (
        0.5 * (1.0 + lax.erf(preact_f * inv_root_two))
        + preact_f * jnp.exp(-0.5 * preact_f * preact_f) * inv_root_tau
    )
    return (upstream.astype(jnp.float32) * derivative).astype(jnp.bfloat16)


def cross_dot(left, right):
    return lax.dot_general(
        left, right, (((1,), (1,)), ((), ())), preferred_element_type=jnp.float32
    )


def exchange(value, axes):
    return lax.all_to_all(value, axes, 0, 0, tiled=True)


def per_device(
    train_input, train_preact, train_upstream, valid_input, valid_preact, valid_upstream
):
    valid_grad = output_grad(valid_preact, valid_upstream)
    valid = jnp.concatenate([valid_input, valid_grad], axis=1)
    rows, width = valid.shape
    dp = lax.axis_size(DP)
    valid_all = jnp.broadcast_to(valid[None], (dp, rows, width)).reshape(dp * rows, width)
    valid_all = exchange(valid_all, DP)
    train_grad = output_grad(train_preact, train_upstream)
    split = valid_input.shape[1]
    input_part = cross_dot(train_input, valid_all[:, :split]) * (1.0 / math.sqrt(D))
    grad_part = cross_dot(train_grad, valid_all[:, split:]) * (1.0 / math.sqrt(FF))
    parts = jnp.concatenate([input_part, grad_part], axis=1)
    tensor = lax.axis_size(TENSOR)
    count, wide = parts.shape
    parts = exchange(parts, TENSOR).reshape(tensor, count // tensor, wide)
    parts = jnp.sum(parts, axis=0)
    product = parts[:, : wide // 2] * parts[:, wide // 2 :]
    sums = jnp.sum(product.reshape(-1, VAL_SEQS, SEQ_LEN), axis=(0, 2)) * (1.0 / SEQ_LEN)
    lanes = jnp.pad(sums, (0, 128 - VAL_SEQS))[None]
    halves = lax.axis_size("yh")
    column = exchange(jnp.broadcast_to(lanes, (halves * tensor, 128)), ("yh",) + TENSOR)
    by_half = jnp.sum(column.reshape(halves, tensor, 128), axis=1)
    first_order = lax.dynamic_slice(by_half, (lax.axis_index("yh"), 0), (1, VAL_SEQS))
    total = jnp.sum(by_half, axis=0, keepdims=True)
    plane = lax.axis_size(("z", "x"))
    planes = exchange(jnp.broadcast_to(total, (plane, 128)), ("z", "x"))
    weight = jnp.sum(planes, axis=0, keepdims=True)[:, :VAL_SEQS]
    second_order = jnp.sum(first_order * weight, axis=1)
    return (first_order, second_order)


def solution(mesh):
    fine = Mesh(mesh.devices.reshape(SIZES), DP + TENSOR)
    return jax.shard_map(
        per_device,
        mesh=fine,
        in_specs=(P(DP, TENSOR),) * 6,
        out_specs=(P(DP, None), P(DP)),
        check_vma=False,
    )
```

```python
import math

import jax
import jax.numpy as jnp
from jax import lax
from jax.sharding import Mesh, PartitionSpec as P

D = 5120
FF = 20480
SEQ_LEN = 256
VAL_SEQS = 2
DP = ("yh", "z", "x")
TENSOR = ("yl", "core")
YH, Z, X, YL, CORE = SIZES = (2, 8, 4, 4, 2)
CLASSES = 4

inv_root_two = 0.7071067811865476
inv_root_tau = 0.3989422804014327


def output_grad(preact, upstream):
    preact_f = preact.astype(jnp.float32)
    derivative = (
        0.5 * (1.0 + lax.erf(preact_f * inv_root_two))
        + preact_f * jnp.exp(-0.5 * preact_f * preact_f) * inv_root_tau
    )
    return (upstream.astype(jnp.float32) * derivative).astype(jnp.bfloat16)


def cross_dot(left, right):
    return lax.dot_general(
        left, right, (((1,), (1,)), ((), ())), preferred_element_type=jnp.float32
    )


def exchange(value, axes, groups=None):
    return lax.all_to_all(value, axes, 0, 0, axis_index_groups=groups, tiled=True)


def place(yh, z, x):
    return (yh * Z + z % Z) * X + x % X


def class_groups():
    return [
        [place(yh, z, kind - 2 * z) for yh in range(YH) for z in range(Z)]
        for kind in range(CLASSES)
    ]


def shift(value, dz, dx):
    pairs = [
        (place(yh, z, x), place(yh, z + dz, x + dx))
        for yh in range(YH)
        for z in range(Z)
        for x in range(X)
    ]
    return lax.ppermute(value, DP, pairs)


def gather_valid(valid):
    rows, width = valid.shape
    members = YH * Z
    own = jnp.broadcast_to(valid[None], (members, rows, width)).reshape(members * rows, width)
    own = exchange(own, DP, class_groups())
    half = own.shape[0] // 2
    return [
        own,
        shift(own, 0, 1),
        shift(own, 0, -1),
        shift(own[:half], 1, 0),
        shift(own[half:], -1, 0),
    ]


def per_device(
    train_input, train_preact, train_upstream, valid_input, valid_preact, valid_upstream
):
    valid_grad = output_grad(valid_preact, valid_upstream)
    blocks = gather_valid(jnp.concatenate([valid_input, valid_grad], axis=1))
    train_grad = lax.optimization_barrier(output_grad(train_preact, train_upstream))
    split = valid_input.shape[1]
    input_parts = [cross_dot(train_input, b[:, :split]) * (1.0 / math.sqrt(D)) for b in blocks]
    grad_parts = [cross_dot(train_grad, b[:, split:]) * (1.0 / math.sqrt(FF)) for b in blocks]
    parts = jnp.concatenate(input_parts + grad_parts, axis=1)
    count, wide = parts.shape
    core = lax.axis_index("core")
    part_rows = count // CORE
    kept = lax.dynamic_slice(parts, (core * part_rows, 0), (part_rows, wide))
    sent = lax.dynamic_slice(parts, ((1 - core) * part_rows, 0), (part_rows, wide))
    parts = kept + lax.ppermute(sent, "core", [(0, 1), (1, 0)])
    parts = exchange(parts, "yl").reshape(YL, part_rows // YL, wide)
    parts = jnp.sum(parts, axis=0)
    product = jnp.sum(parts[:, : wide // 2] * parts[:, wide // 2 :], axis=0)
    edge = blocks[0].shape[0] // 2
    sums = jnp.sum(product.reshape(-1, VAL_SEQS, edge), axis=(0, 2)) * (1.0 / SEQ_LEN)
    lanes = jnp.pad(sums, (0, 128 - VAL_SEQS))[None]
    tensor = YL * CORE
    column = exchange(jnp.broadcast_to(lanes, (YH * tensor, 128)), ("yh",) + TENSOR)
    by_half = jnp.sum(column.reshape(YH, tensor, 128), axis=1)
    first_order = lax.dynamic_slice(by_half, (lax.axis_index("yh"), 0), (1, VAL_SEQS))
    total = jnp.sum(by_half, axis=0, keepdims=True)
    plane = Z * X
    planes = exchange(jnp.broadcast_to(total, (plane, 128)), ("z", "x"))
    weight = jnp.sum(planes, axis=0, keepdims=True)[:, :VAL_SEQS]
    second_order = jnp.sum(first_order * weight, axis=1)
    return (first_order, second_order)


def solution(mesh):
    fine = Mesh(mesh.devices.reshape(SIZES), DP + TENSOR)
    return jax.shard_map(
        per_device,
        mesh=fine,
        in_specs=(P(DP, TENSOR),) * 6,
        out_specs=(P(DP, None), P(DP)),
        check_vma=False,
    )
```

```python
import math

import jax
import jax.numpy as jnp
from jax import lax
from jax.sharding import Mesh, PartitionSpec as P

D = 5120
FF = 20480
SEQ_LEN = 256
VAL_SEQS = 2
DP = ("yh", "z", "x")
TENSOR = ("yl", "core")
YH, Z, X, YL, CORE = SIZES = (2, 8, 4, 4, 2)
CLASSES = 4

inv_root_two = 0.7071067811865476
inv_root_tau = 0.3989422804014327


def output_grad(preact, upstream):
    preact_f = preact.astype(jnp.float32)
    derivative = (
        0.5 * (1.0 + lax.erf(preact_f * inv_root_two))
        + preact_f * jnp.exp(-0.5 * preact_f * preact_f) * inv_root_tau
    )
    return (upstream.astype(jnp.float32) * derivative).astype(jnp.bfloat16)


def cross_dot(left, right):
    return lax.dot_general(
        left, right, (((1,), (1,)), ((), ())), preferred_element_type=jnp.float32
    )


def exchange(value, axes, groups=None):
    return lax.all_to_all(value, axes, 0, 0, axis_index_groups=groups, tiled=True)


def place(yh, z, x):
    return (yh * Z + z % Z) * X + x % X


def class_groups():
    return [
        [place(yh, z, kind - 2 * z) for yh in range(YH) for z in range(Z)]
        for kind in range(CLASSES)
    ]


def shift(value, dz, dx):
    pairs = [
        (place(yh, z, x), place(yh, z + dz, x + dx))
        for yh in range(YH)
        for z in range(Z)
        for x in range(X)
    ]
    return lax.ppermute(value, DP, pairs)


def class_gather(valid):
    rows, width = valid.shape
    members = YH * Z
    own = jnp.broadcast_to(valid[None], (members, rows, width)).reshape(members * rows, width)
    return exchange(own, DP, class_groups())


def neighbour_blocks(own):
    half = own.shape[0] // 2
    right, left = shift(own, 0, 1), shift(own, 0, -1)
    above, below = shift(own[:half], 1, 0), shift(own[half:], -1, 0)
    return [[own], [above, below], [right], [left]]


def per_device(
    train_input, train_preact, train_upstream, valid_input, valid_preact, valid_upstream
):
    valid_grad = output_grad(valid_preact, valid_upstream)
    own = class_gather(jnp.concatenate([valid_input, valid_grad], axis=1))
    own, train_preact, train_upstream = lax.optimization_barrier(
        (own, train_preact, train_upstream)
    )
    columns = neighbour_blocks(own)
    train_grad = lax.optimization_barrier(output_grad(train_preact, train_upstream))
    split = valid_input.shape[1]
    parts = []
    for column in columns:
        parts += [cross_dot(train_input, b[:, :split]) * (1.0 / math.sqrt(D)) for b in column]
        parts += [cross_dot(train_grad, b[:, split:]) * (1.0 / math.sqrt(FF)) for b in column]
    parts = jnp.concatenate(parts, axis=1)
    count, wide = parts.shape
    core = lax.axis_index("core")
    part_rows = count // CORE
    kept = lax.dynamic_slice(parts, (core * part_rows, 0), (part_rows, wide))
    sent = lax.dynamic_slice(parts, ((1 - core) * part_rows, 0), (part_rows, wide))
    parts = kept + lax.ppermute(sent, "core", [(0, 1), (1, 0)])
    parts = exchange(parts, "yl").reshape(YL, part_rows // YL, wide)
    parts = jnp.sum(parts, axis=0)
    pairs = parts.reshape(-1, CLASSES, 2, VAL_SEQS, wide // (4 * CLASSES))
    sums = jnp.sum(pairs[:, :, 0] * pairs[:, :, 1], axis=(0, 1, 3)) * (1.0 / SEQ_LEN)
    lanes = jnp.pad(sums, (0, 128 - VAL_SEQS))[None]
    tensor = YL * CORE
    lanes, yh = lax.optimization_barrier((lanes, lax.axis_index("yh")))
    column = exchange(jnp.broadcast_to(lanes, (YH * tensor, 128)), ("yh",) + TENSOR)
    by_half = jnp.sum(column.reshape(YH, tensor, 128), axis=1)
    first_order = lax.dynamic_slice(by_half, (yh, 0), (1, VAL_SEQS))
    total = jnp.sum(by_half, axis=0, keepdims=True)
    first_order, total = lax.optimization_barrier((first_order, total))
    plane = Z * X
    planes = exchange(jnp.broadcast_to(total, (plane, 128)), ("z", "x"))
    weight = jnp.sum(planes, axis=0, keepdims=True)[:, :VAL_SEQS]
    second_order = jnp.sum(first_order * weight, axis=1)
    return (first_order, second_order)


def solution(mesh):
    fine = Mesh(mesh.devices.reshape(SIZES), DP + TENSOR)
    return jax.shard_map(
        per_device,
        mesh=fine,
        in_specs=(P(DP, TENSOR),) * 6,
        out_specs=(P(DP, None), P(DP)),
        check_vma=False,
    )
```

```python
import math

import jax
import jax.numpy as jnp
from jax import lax
from jax.experimental import pallas as pl
from jax.sharding import Mesh, PartitionSpec as P

D = 5120
FF = 20480
SEQ_LEN = 256
VAL_SEQS = 2
DP = ("yh", "z", "x")
TENSOR = ("yl", "core")
YH, Z, X, YL, CORE = SIZES = (2, 8, 4, 4, 2)
CLASSES = 4
LANES = 128
LOW, HIGH = -126.0, 30.0

inv_root_two = 0.7071067811865476
inv_root_tau = 0.3989422804014327


def output_grad(preact, upstream):
    preact_f = preact.astype(jnp.float32)
    derivative = (
        0.5 * (1.0 + lax.erf(preact_f * inv_root_two))
        + preact_f * jnp.exp(-0.5 * preact_f * preact_f) * inv_root_tau
    )
    return (upstream.astype(jnp.float32) * derivative).astype(jnp.bfloat16)


def cross_dot(left, right):
    return lax.dot_general(
        left, right, (((1,), (1,)), ((), ())), preferred_element_type=jnp.float32
    )


def exchange(value, axes, groups=None):
    return lax.all_to_all(value, axes, 0, 0, axis_index_groups=groups, tiled=True)


def place(yh, z, x):
    return (yh * Z + z % Z) * X + x % X


def class_groups():
    return [
        [place(yh, z, kind - 2 * z) for yh in range(YH) for z in range(Z)]
        for kind in range(CLASSES)
    ]


def shift(value, dz, dx):
    pairs = [
        (place(yh, z, x), place(yh, z + dz, x + dx))
        for yh in range(YH)
        for z in range(Z)
        for x in range(X)
    ]
    return lax.ppermute(value, DP, pairs)


def valid_copies_kernel(input_ref, preact_ref, upstream_ref, out_ref):
    split = input_ref.shape[1]
    joined = output_grad(preact_ref[...], upstream_ref[...])
    for member in range(out_ref.shape[0]):
        out_ref[member, :, :split] = input_ref[...]
        out_ref[member, :, split:] = joined


def class_gather(valid_input, valid_preact, valid_upstream):
    rows, split = valid_input.shape
    width = split + valid_preact.shape[1]
    members = YH * Z
    copies = pl.pallas_call(
        valid_copies_kernel,
        out_shape=jax.ShapeDtypeStruct((members, rows, width), jnp.bfloat16),
    )(valid_input, valid_preact, valid_upstream)
    return exchange(copies.reshape(members * rows, width), DP, class_groups())


def neighbour_blocks(own):
    half = own.shape[0] // 2
    right, left = shift(own, 0, 1), shift(own, 0, -1)
    above, below = shift(own[:half], 1, 0), shift(own[half:], -1, 0)
    return [[own], [above, below], [right], [left]]


def encode(parts):
    kinds = [parts[0::2], parts[1::2]]
    largest = jnp.stack(
        [jnp.max(jnp.stack([jnp.max(jnp.abs(p), axis=1) for p in kind]), axis=0) for kind in kinds],
        axis=1,
    )
    exponents = jnp.clip(jnp.ceil(jnp.log2(jnp.maximum(largest, 2.0**LOW))), LOW, HIGH)
    scale = jnp.exp2(-exponents)
    scaled = [(p * scale[:, i % 2, None]).astype(jnp.float16) for i, p in enumerate(parts)]
    tail = jnp.pad(exponents, ((0, 0), (0, LANES - 2))).astype(jnp.float16)
    return jnp.concatenate(scaled + [tail], axis=1)


def decode(coded):
    blocks = 2 * CLASSES
    scale = jnp.exp2(coded[:, :, blocks * LANES : blocks * LANES + 2].astype(jnp.float32))
    return [
        jnp.sum(
            coded[:, :, i * LANES : (i + 1) * LANES].astype(jnp.float32)
            * scale[:, :, i % 2, None],
            axis=0,
        )
        for i in range(blocks)
    ]


def finish_kernel(column_ref, planes_ref, first_ref, second_ref):
    tensor = YL * CORE
    start = pl.multiple_of(lax.axis_index("yh") * tensor, tensor)
    first = jnp.sum(column_ref[pl.ds(start, tensor), :], axis=0, keepdims=True)
    weight = jnp.sum(planes_ref[...], axis=0, keepdims=True)
    first_ref[...] = first[:, :VAL_SEQS]
    second_ref[...] = jnp.sum(first * weight, axis=1, keepdims=True)


def per_device(
    train_input, train_preact, train_upstream, valid_input, valid_preact, valid_upstream
):
    own = class_gather(valid_input, valid_preact, valid_upstream)
    own, train_preact, train_upstream = lax.optimization_barrier(
        (own, train_preact, train_upstream)
    )
    columns = neighbour_blocks(own)
    train_grad = lax.optimization_barrier(output_grad(train_preact, train_upstream))
    split = valid_input.shape[1]
    parts = []
    for column in columns:
        inputs = [cross_dot(train_input, b[:, :split]) * (1.0 / math.sqrt(D)) for b in column]
        grads = [cross_dot(train_grad, b[:, split:]) * (1.0 / math.sqrt(FF)) for b in column]
        parts += [jnp.concatenate(inputs, axis=1), jnp.concatenate(grads, axis=1)]
    coded = encode(parts)
    tensor = YL * CORE
    coded = exchange(coded, TENSOR).reshape(tensor, -1, coded.shape[1])
    summed = decode(coded)
    product = sum(summed[2 * i] * summed[2 * i + 1] for i in range(CLASSES))
    product = jnp.sum(product, axis=0).reshape(VAL_SEQS, LANES // VAL_SEQS)
    sums = jnp.sum(product, axis=1) * (1.0 / SEQ_LEN)
    lanes = jnp.pad(sums, (0, LANES - VAL_SEQS))[None]
    column = exchange(jnp.broadcast_to(lanes, (YH * tensor, LANES)), ("yh",) + TENSOR)
    total = jnp.sum(column, axis=0, keepdims=True)
    planes = exchange(jnp.broadcast_to(total, (Z * X, LANES)), ("z", "x"))
    first_order, second_order = pl.pallas_call(
        finish_kernel,
        out_shape=(
            jax.ShapeDtypeStruct((1, VAL_SEQS), jnp.float32),
            jax.ShapeDtypeStruct((1, 1), jnp.float32),
        ),
    )(column, planes)
    return (first_order, second_order.reshape(1))


def solution(mesh):
    fine = Mesh(mesh.devices.reshape(SIZES), DP + TENSOR)
    return jax.shard_map(
        per_device,
        mesh=fine,
        in_specs=(P(DP, TENSOR),) * 6,
        out_specs=(P(DP, None), P(DP)),
        check_vma=False,
    )
```

```python
import math

import jax
import jax.numpy as jnp
from jax import lax
from jax.experimental import pallas as pl
from jax.sharding import Mesh, PartitionSpec as P

D = 5120
FF = 20480
SEQ_LEN = 256
VAL_SEQS = 2
DP = ("yh", "z", "x")
TENSOR = ("yl", "core")
YH, Z, X, YL, CORE = SIZES = (2, 8, 4, 4, 2)
CLASSES = 4
LANES = 128
LOW, HIGH = -126.0, 30.0

inv_root_two = 0.7071067811865476
inv_root_tau = 0.3989422804014327


def output_grad(preact, upstream):
    preact_f = preact.astype(jnp.float32)
    derivative = (
        0.5 * (1.0 + lax.erf(preact_f * inv_root_two))
        + preact_f * jnp.exp(-0.5 * preact_f * preact_f) * inv_root_tau
    )
    return (upstream.astype(jnp.float32) * derivative).astype(jnp.bfloat16)


def cross_dot(left, right):
    return lax.dot_general(
        left, right, (((1,), (1,)), ((), ())), preferred_element_type=jnp.float32
    )


def exchange(value, axes, groups=None):
    return lax.all_to_all(value, axes, 0, 0, axis_index_groups=groups, tiled=True)


def place(yh, z, x):
    return (yh * Z + z % Z) * X + x % X


def class_groups():
    return [
        [place(yh, z, kind - 2 * z) for yh in range(YH) for z in range(Z)]
        for kind in range(CLASSES)
    ]


def shift(value, dz, dx):
    pairs = [
        (place(yh, z, x), place(yh, z + dz, x + dx))
        for yh in range(YH)
        for z in range(Z)
        for x in range(X)
    ]
    return lax.ppermute(value, DP, pairs)


def valid_copies_kernel(input_ref, preact_ref, upstream_ref, out_ref, mine_ref):
    tensor = YL * CORE
    member = lax.broadcasted_iota(jnp.int32, mine_ref.shape, 0)
    mine_ref[...] = (member // tensor == lax.axis_index("yh")).astype(jnp.float32)
    split = input_ref.shape[1]
    joined = output_grad(preact_ref[...], upstream_ref[...])
    for member in range(out_ref.shape[0]):
        out_ref[member, :, :split] = input_ref[...]
        out_ref[member, :, split:] = joined


def class_gather(valid_input, valid_preact, valid_upstream):
    rows, split = valid_input.shape
    width = split + valid_preact.shape[1]
    members = YH * Z
    copies, mine = pl.pallas_call(
        valid_copies_kernel,
        out_shape=(
            jax.ShapeDtypeStruct((members, rows, width), jnp.bfloat16),
            jax.ShapeDtypeStruct((YH * YL * CORE, LANES), jnp.float32),
        ),
    )(valid_input, valid_preact, valid_upstream)
    return exchange(copies.reshape(members * rows, width), DP, class_groups()), mine


def neighbour_blocks(own):
    half = own.shape[0] // 2
    right, left = shift(own, 0, 1), shift(own, 0, -1)
    above, below = shift(own[:half], 1, 0), shift(own[half:], -1, 0)
    return [[own], [above, below], [right], [left]]


def encode(parts):
    kinds = [parts[0::2], parts[1::2]]
    largest = jnp.stack(
        [jnp.max(jnp.stack([jnp.max(jnp.abs(p), axis=1) for p in kind]), axis=0) for kind in kinds],
        axis=1,
    )
    exponents = jnp.clip(jnp.ceil(jnp.log2(jnp.maximum(largest, 2.0**LOW))), LOW, HIGH)
    scale = jnp.exp2(-exponents)
    scaled = [(p * scale[:, i % 2, None]).astype(jnp.float16) for i, p in enumerate(parts)]
    tail = jnp.pad(exponents, ((0, 0), (0, LANES - 2))).astype(jnp.float16)
    return jnp.concatenate(scaled + [tail], axis=1)


def decode(coded):
    blocks = 2 * CLASSES
    scale = jnp.exp2(coded[:, :, blocks * LANES : blocks * LANES + 2].astype(jnp.float32))
    return [
        jnp.sum(
            coded[:, :, i * LANES : (i + 1) * LANES].astype(jnp.float32)
            * scale[:, :, i % 2, None],
            axis=0,
        )
        for i in range(blocks)
    ]


def per_device(
    train_input, train_preact, train_upstream, valid_input, valid_preact, valid_upstream
):
    own, mine = class_gather(valid_input, valid_preact, valid_upstream)
    own, train_preact, train_upstream = lax.optimization_barrier(
        (own, train_preact, train_upstream)
    )
    columns = neighbour_blocks(own)
    train_grad = lax.optimization_barrier(output_grad(train_preact, train_upstream))
    split = valid_input.shape[1]
    parts = []
    for column in columns:
        parts += [cross_dot(train_input, b[:, :split]) * (1.0 / math.sqrt(D)) for b in column]
        parts += [cross_dot(train_grad, b[:, split:]) * (1.0 / math.sqrt(FF)) for b in column]
    parts = jnp.concatenate(parts, axis=1)
    wide = parts.shape[1]
    parts = jnp.sum(exchange(parts, "core").reshape(CORE, -1, wide), axis=0)
    blocks = [parts[:, i : i + LANES] for i in range(0, wide, LANES)]
    coded = encode(blocks)
    coded = exchange(coded, "yl").reshape(YL, -1, coded.shape[1])
    summed = decode(coded)
    product = sum(summed[2 * i] * summed[2 * i + 1] for i in range(CLASSES))
    product = jnp.sum(product, axis=0).reshape(VAL_SEQS, LANES // VAL_SEQS)
    sums = jnp.sum(product, axis=1) * (1.0 / SEQ_LEN)
    lanes = jnp.pad(sums, (0, LANES - VAL_SEQS))[None]
    column = exchange(jnp.broadcast_to(lanes, mine.shape), ("yh",) + TENSOR)
    first = jnp.sum(column * mine, axis=0, keepdims=True)
    total = first + jnp.sum(column * (1.0 - mine), axis=0, keepdims=True)
    planes = exchange(jnp.broadcast_to(total, (Z * X, LANES)), ("z", "x"))
    weight = jnp.sum(planes, axis=0, keepdims=True)
    return (first[:, :VAL_SEQS], jnp.sum(first * weight, axis=1))


def solution(mesh):
    fine = Mesh(mesh.devices.reshape(SIZES), DP + TENSOR)
    return jax.shard_map(
        per_device,
        mesh=fine,
        in_specs=(P(DP, TENSOR),) * 6,
        out_specs=(P(DP, None), P(DP)),
        check_vma=False,
    )
```

```python
import math

import jax
import jax.numpy as jnp
from jax import lax
from jax.experimental import pallas as pl
from jax.sharding import Mesh, PartitionSpec as P

D = 5120
FF = 20480
SEQ_LEN = 256
VAL_SEQS = 2
DP = ("yh", "z", "x")
TENSOR = ("yl", "core")
YH, Z, X, YL, CORE = SIZES = (2, 8, 4, 4, 2)
CLASSES = 4
LANES = 128
TAIL = 8
LOW, HIGH = -126.0, 30.0

inv_root_two = 0.7071067811865476
inv_root_tau = 0.3989422804014327


def output_grad(preact, upstream):
    preact_f = preact.astype(jnp.float32)
    derivative = (
        0.5 * (1.0 + lax.erf(preact_f * inv_root_two))
        + preact_f * jnp.exp(-0.5 * preact_f * preact_f) * inv_root_tau
    )
    return (upstream.astype(jnp.float32) * derivative).astype(jnp.bfloat16)


def cross_dot(left, right):
    return lax.dot_general(
        left, right, (((1,), (1,)), ((), ())), preferred_element_type=jnp.float32
    )


def exchange(value, axes, groups=None):
    return lax.all_to_all(value, axes, 0, 0, axis_index_groups=groups, tiled=True)


def place(yh, z, x):
    return (yh * Z + z % Z) * X + x % X


def device(yh, z, x, yl, core):
    return (((yh * Z + z % Z) * X + x % X) * YL + yl) * CORE + core


def class_groups():
    groups = []
    for kind in range(CLASSES):
        for yl in range(YL):
            groups.append(
                [device(yh, z, kind - 2 * z, yl, 0) for yh in range(YH) for z in range(Z)]
            )
            groups.append(
                [
                    device(yh, (kind - 2 * x) % 4 + 4 * far, x, yl, 1)
                    for yh in range(YH)
                    for x in range(X)
                    for far in range(2)
                ]
            )
    return groups


def shift(value, major, minor):
    pairs = []
    for yh in range(YH):
        for z in range(Z):
            for x in range(X):
                for yl in range(YL):
                    pairs.append(
                        (device(yh, z, x, yl, 0), device(yh, z + minor, x + major, yl, 0))
                    )
                    pairs.append(
                        (device(yh, z, x, yl, 1), device(yh, z + major, x + minor, yl, 1))
                    )
    return lax.ppermute(value, DP + TENSOR, pairs)


def valid_copies_kernel(input_ref, preact_ref, upstream_ref, out_ref, mine_ref):
    tensor = YL * CORE
    member = lax.broadcasted_iota(jnp.int32, mine_ref.shape, 0)
    mine_ref[...] = (member // tensor == lax.axis_index("yh")).astype(jnp.float32)
    split = input_ref.shape[1]
    joined = output_grad(preact_ref[...], upstream_ref[...])
    for member in range(out_ref.shape[0]):
        out_ref[member, :, :split] = input_ref[...]
        out_ref[member, :, split:] = joined


def class_gather(valid_input, valid_preact, valid_upstream):
    rows, split = valid_input.shape
    width = split + valid_preact.shape[1]
    members = YH * Z
    copies, mine = pl.pallas_call(
        valid_copies_kernel,
        out_shape=(
            jax.ShapeDtypeStruct((members, rows, width), jnp.bfloat16),
            jax.ShapeDtypeStruct((YH * YL * CORE, LANES), jnp.float32),
        ),
    )(valid_input, valid_preact, valid_upstream)
    return exchange(
        copies.reshape(members * rows, width), DP + TENSOR, class_groups()
    ), mine


def neighbour_blocks(own):
    half = own.shape[0] // 2
    back, on = shift(own, 1, 0), shift(own, -1, 0)
    across = [shift(own[:half], 0, 1), shift(own[half:], 0, -1)]
    return [own, jnp.concatenate(across), back, on]


def align_kernel(pieces_ref, out_ref):
    z, x = lax.axis_index("z"), lax.axis_index("x")
    tile = out_ref.shape[0] // (CLASSES * 2 * YH * Z)
    for place0, step in enumerate((0, 2, 3, 1)):
        for source_z in range(Z):
            source_x = (x + 2 * z + step - 2 * source_z + 16) & 3
            turn = (2 * source_x + source_z - 2 * x - z + 16) & 3
            place1 = jnp.where(turn == 1, 3, jnp.where(turn == 2, 1, jnp.where(turn == 3, 2, 0)))
            other = place1 * (2 * YH * Z) + 2 * source_x + source_z // 4
            for part in range(2 * YH):
                here = (place0 * 2 * YH * Z + part * Z + source_z) * tile
                there = pl.multiple_of((other + part * Z) * tile, tile)
                out_ref[here : here + tile, :] = (
                    pieces_ref[0, here : here + tile, :] + pieces_ref[1, pl.ds(there, tile), :]
                )


def encode(parts):
    largest = jnp.max(jnp.abs(parts), axis=2)
    exponents = jnp.clip(jnp.ceil(jnp.log2(jnp.maximum(largest, 2.0**LOW))), LOW, HIGH)
    scaled = (parts * jnp.exp2(-exponents)[:, :, None]).astype(jnp.float16)
    blocks, kinds, rows, lanes = parts.shape
    tail = jnp.pad(exponents, ((0, 0), (0, TAIL - kinds), (0, 0))).astype(jnp.float16)
    return jnp.concatenate([scaled.reshape(blocks, kinds * rows, lanes), tail], axis=1)


def decode(coded, kinds):
    count, rows, lanes = coded.shape
    rows -= TAIL
    scale = jnp.exp2(coded[:, rows : rows + kinds].astype(jnp.float32))
    values = coded[:, :rows].astype(jnp.float32).reshape(count, kinds, rows // kinds, lanes)
    return jnp.sum(values * scale[:, :, None], axis=0)


def per_device(
    train_input, train_preact, train_upstream, valid_input, valid_preact, valid_upstream
):
    own, mine = class_gather(valid_input, valid_preact, valid_upstream)
    own, train_preact, train_upstream = lax.optimization_barrier(
        (own, train_preact, train_upstream)
    )
    blocks = neighbour_blocks(own)
    train_grad = lax.optimization_barrier(output_grad(train_preact, train_upstream))
    split = valid_input.shape[1]
    parts = []
    for block in blocks:
        parts.append(cross_dot(block[:, :split], train_input) * (1.0 / math.sqrt(D)))
        parts.append(cross_dot(block[:, split:], train_grad) * (1.0 / math.sqrt(FF)))
    parts = jnp.concatenate(parts)
    rows = parts.shape[0]
    pieces = jnp.stack(jnp.split(parts, CORE, axis=1))
    pieces = exchange(pieces, "core")
    parts = pl.pallas_call(
        align_kernel,
        out_shape=jax.ShapeDtypeStruct(pieces.shape[1:], jnp.float32),
    )(pieces)
    coded = encode(parts.reshape(CLASSES, 2, rows // (2 * CLASSES), -1))
    input_kernel, grad_kernel = decode(exchange(coded, "yl"), 2)
    product = (input_kernel * grad_kernel).reshape(VAL_SEQS, -1, input_kernel.shape[1])
    sums = jnp.sum(product, axis=(1, 2)) * (1.0 / SEQ_LEN)
    lanes = jnp.pad(sums, (0, LANES - VAL_SEQS))[None]
    column = exchange(jnp.broadcast_to(lanes, mine.shape), ("yh",) + TENSOR)
    first = jnp.sum(column * mine, axis=0, keepdims=True)
    total = first + jnp.sum(column * (1.0 - mine), axis=0, keepdims=True)
    planes = exchange(jnp.broadcast_to(total, (Z * X, LANES)), ("z", "x"))
    weight = jnp.sum(planes, axis=0, keepdims=True)
    return (first[:, :VAL_SEQS], jnp.sum(first * weight, axis=1))


def solution(mesh):
    fine = Mesh(mesh.devices.reshape(SIZES), DP + TENSOR)
    return jax.shard_map(
        per_device,
        mesh=fine,
        in_specs=(P(DP, TENSOR),) * 6,
        out_specs=(P(DP, None), P(DP)),
        check_vma=False,
    )
```

```python
import math

import jax
import jax.numpy as jnp
from jax import lax
from jax.experimental import pallas as pl
from jax.sharding import Mesh, PartitionSpec as P

D = 5120
FF = 20480
SEQ_LEN = 256
VAL_SEQS = 2
DP = ("yh", "z", "x")
TENSOR = ("yl", "core")
YH, Z, X, YL, CORE = SIZES = (2, 8, 4, 4, 2)
CLASSES = 4
LANES = 128
TAIL = 8
LOW, HIGH = -126.0, 30.0

inv_root_two = 0.7071067811865476
inv_root_tau = 0.3989422804014327


def output_grad(preact, upstream):
    preact_f = preact.astype(jnp.float32)
    derivative = (
        0.5 * (1.0 + lax.erf(preact_f * inv_root_two))
        + preact_f * jnp.exp(-0.5 * preact_f * preact_f) * inv_root_tau
    )
    return (upstream.astype(jnp.float32) * derivative).astype(jnp.bfloat16)


def cross_dot(left, right):
    return lax.dot_general(
        left, right, (((1,), (1,)), ((), ())), preferred_element_type=jnp.float32
    )


def exchange(value, axes, groups=None):
    return lax.all_to_all(value, axes, 0, 0, axis_index_groups=groups, tiled=True)


def place(yh, z, x):
    return (yh * Z + z % Z) * X + x % X


def class_groups():
    return [
        [place(yh, z, kind - 2 * z) for yh in range(YH) for z in range(Z)]
        for kind in range(CLASSES)
    ]


def shift(value, dz, dx):
    pairs = [
        (place(yh, z, x), place(yh, z + dz, x + dx))
        for yh in range(YH)
        for z in range(Z)
        for x in range(X)
    ]
    return lax.ppermute(value, DP, pairs)


def valid_copies_kernel(input_ref, preact_ref, upstream_ref, out_ref, mine_ref):
    tensor = YL * CORE
    member = lax.broadcasted_iota(jnp.int32, mine_ref.shape, 0)
    mine_ref[...] = (member // tensor == lax.axis_index("yh")).astype(jnp.float32)
    split = input_ref.shape[1]
    joined = output_grad(preact_ref[...], upstream_ref[...])
    for member in range(out_ref.shape[0]):
        out_ref[member, :, :split] = input_ref[...]
        out_ref[member, :, split:] = joined


def class_gather(valid_input, valid_preact, valid_upstream):
    rows, split = valid_input.shape
    width = split + valid_preact.shape[1]
    members = YH * Z
    copies, mine = pl.pallas_call(
        valid_copies_kernel,
        out_shape=(
            jax.ShapeDtypeStruct((members, rows, width), jnp.bfloat16),
            jax.ShapeDtypeStruct((YH * YL * CORE, LANES), jnp.float32),
        ),
    )(valid_input, valid_preact, valid_upstream)
    return exchange(copies.reshape(members * rows, width), DP, class_groups()), mine


def neighbour_rows(own):
    half = own.shape[0] // 2
    right, left = shift(own, 0, 1), shift(own, 0, -1)
    above, below = shift(own[:half], 1, 0), shift(own[half:], -1, 0)
    return jnp.concatenate([above, below, right, left])


def encode(parts):
    kinds, blocks, rows, lanes = parts.shape
    largest = jnp.max(jnp.abs(parts), axis=2)
    exponents = jnp.clip(jnp.ceil(jnp.log2(jnp.maximum(largest, 2.0**LOW))), LOW, HIGH)
    scale = jnp.exp2(-exponents)[:, :, None]
    scaled = [(parts[kind] * scale[kind]).astype(jnp.float16) for kind in range(kinds)]
    tail = jnp.pad(exponents.transpose(1, 0, 2), ((0, 0), (0, TAIL - kinds), (0, 0)))
    return jnp.concatenate(scaled + [tail.astype(jnp.float16)], axis=1)


def decode(coded, kinds):
    count, rows, lanes = coded.shape
    rows -= TAIL
    scale = jnp.exp2(coded[:, rows : rows + kinds].astype(jnp.float32))
    values = coded[:, :rows].astype(jnp.float32).reshape(count, kinds, rows // kinds, lanes)
    return jnp.sum(values * scale[:, :, None], axis=0)


def per_device(
    train_input, train_preact, train_upstream, valid_input, valid_preact, valid_upstream
):
    own, mine = class_gather(valid_input, valid_preact, valid_upstream)
    own, train_preact, train_upstream = lax.optimization_barrier(
        (own, train_preact, train_upstream)
    )
    foreign = neighbour_rows(own)
    train_grad = lax.optimization_barrier(output_grad(train_preact, train_upstream))
    split = valid_input.shape[1]
    input_scale, grad_scale = 1.0 / math.sqrt(D), 1.0 / math.sqrt(FF)
    parts = [cross_dot(rows[:, :split], train_input) * input_scale for rows in (own, foreign)]
    parts += [cross_dot(rows[:, split:], train_grad) * grad_scale for rows in (own, foreign)]
    pieces = jnp.stack(jnp.split(jnp.concatenate(parts), CORE, axis=1))
    parts = jnp.sum(exchange(pieces, "core"), axis=0)
    coded = encode(parts.reshape(2, CLASSES, -1, parts.shape[1]))
    input_kernel, grad_kernel = decode(exchange(coded, "yl"), 2)
    product = (input_kernel * grad_kernel).reshape(VAL_SEQS, -1, input_kernel.shape[1])
    sums = jnp.sum(product, axis=(1, 2)) * (1.0 / SEQ_LEN)
    lanes = jnp.pad(sums, (0, LANES - VAL_SEQS))[None]
    column = exchange(jnp.broadcast_to(lanes, mine.shape), ("yh",) + TENSOR)
    first = jnp.sum(column * mine, axis=0, keepdims=True)
    total = first + jnp.sum(column * (1.0 - mine), axis=0, keepdims=True)
    planes = exchange(jnp.broadcast_to(total, (Z * X, LANES)), ("z", "x"))
    weight = jnp.sum(planes, axis=0, keepdims=True)
    return (first[:, :VAL_SEQS], jnp.sum(first * weight, axis=1))


def solution(mesh):
    fine = Mesh(mesh.devices.reshape(SIZES), DP + TENSOR)
    return jax.shard_map(
        per_device,
        mesh=fine,
        in_specs=(P(DP, TENSOR),) * 6,
        out_specs=(P(DP, None), P(DP)),
        check_vma=False,
    )
```

```python
import math

import jax
import jax.numpy as jnp
from jax import lax
from jax.experimental import pallas as pl
from jax.sharding import Mesh, PartitionSpec as P

D = 5120
FF = 20480
SEQ_LEN = 256
VAL_SEQS = 2
DP = ("yh", "z", "x")
TENSOR = ("yl", "core")
YH, Z, X, YL, CORE = SIZES = (2, 8, 4, 4, 2)
CLASSES = 4
LANES = 128
TAIL = 8
LOW, HIGH = -126.0, 30.0

inv_root_two = 0.7071067811865476
inv_root_tau = 0.3989422804014327


def output_grad(preact, upstream):
    preact_f = preact.astype(jnp.float32)
    derivative = (
        0.5 * (1.0 + lax.erf(preact_f * inv_root_two))
        + preact_f * jnp.exp(-0.5 * preact_f * preact_f) * inv_root_tau
    )
    return (upstream.astype(jnp.float32) * derivative).astype(jnp.bfloat16)


def cross_dot(left, right):
    return lax.dot_general(
        left, right, (((1,), (1,)), ((), ())), preferred_element_type=jnp.float32
    )


def exchange(value, axes, groups=None):
    return lax.all_to_all(value, axes, 0, 0, axis_index_groups=groups, tiled=True)


def place(yh, z, x):
    return (yh * Z + z % Z) * X + x % X


def class_groups():
    return [
        [place(yh, z, kind - 2 * z) for yh in range(YH) for z in range(Z)]
        for kind in range(CLASSES)
    ]


def device(yh, z, x, yl, core):
    return (place(yh, z, x) * YL + yl) * CORE + core


def shift(value, dz, dx):
    pairs = [
        (device(yh, z, x, yl, core), device(yh, z + turn * dz, x + turn * dx, yl, core))
        for yh in range(YH)
        for z in range(Z)
        for x in range(X)
        for yl in range(YL)
        for core, turn in enumerate((1, -1))
    ]
    return lax.ppermute(value, DP + TENSOR, pairs)


def valid_copies_kernel(input_ref, preact_ref, upstream_ref, out_ref, mine_ref):
    tensor = YL * CORE
    member = lax.broadcasted_iota(jnp.int32, mine_ref.shape, 0)
    mine_ref[...] = (member // tensor == lax.axis_index("yh")).astype(jnp.float32)
    split = input_ref.shape[1]
    joined = output_grad(preact_ref[...], upstream_ref[...])
    for member in range(out_ref.shape[0]):
        out_ref[member, :, :split] = input_ref[...]
        out_ref[member, :, split:] = joined


def class_gather(valid_input, valid_preact, valid_upstream):
    rows, split = valid_input.shape
    width = split + valid_preact.shape[1]
    members = YH * Z
    copies, mine = pl.pallas_call(
        valid_copies_kernel,
        out_shape=(
            jax.ShapeDtypeStruct((members, rows, width), jnp.bfloat16),
            jax.ShapeDtypeStruct((YH * YL * CORE, LANES), jnp.float32),
        ),
    )(valid_input, valid_preact, valid_upstream)
    return exchange(copies.reshape(members * rows, width), DP, class_groups()), mine


def neighbour_rows(own):
    half = own.shape[0] // 2
    first, second = shift(own, 0, 1), shift(own, 0, -1)
    across = [shift(own[:half], 1, 0), shift(own[half:], -1, 0)]
    return jnp.concatenate(across + [first, second])


def encode(parts):
    kinds, blocks, rows, lanes = parts.shape
    largest = jnp.max(jnp.abs(parts), axis=2)
    exponents = jnp.clip(jnp.ceil(jnp.log2(jnp.maximum(largest, 2.0**LOW))), LOW, HIGH)
    scale = jnp.exp2(-exponents)[:, :, None]
    scaled = [(parts[kind] * scale[kind]).astype(jnp.float16) for kind in range(kinds)]
    tail = jnp.pad(exponents.transpose(1, 0, 2), ((0, 0), (0, TAIL - kinds), (0, 0)))
    return jnp.concatenate(scaled + [tail.astype(jnp.float16)], axis=1)


def decode(coded, kinds):
    count, rows, lanes = coded.shape
    rows -= TAIL
    scale = jnp.exp2(coded[:, rows : rows + kinds].astype(jnp.float32))
    values = coded[:, :rows].astype(jnp.float32).reshape(count, kinds, rows // kinds, lanes)
    return jnp.sum(values * scale[:, :, None], axis=0)


def per_device(
    train_input, train_preact, train_upstream, valid_input, valid_preact, valid_upstream
):
    own, mine = class_gather(valid_input, valid_preact, valid_upstream)
    own, train_preact, train_upstream = lax.optimization_barrier(
        (own, train_preact, train_upstream)
    )
    foreign = neighbour_rows(own)
    train_grad = lax.optimization_barrier(output_grad(train_preact, train_upstream))
    split = valid_input.shape[1]
    input_scale, grad_scale = 1.0 / math.sqrt(D), 1.0 / math.sqrt(FF)
    parts = [cross_dot(rows[:, :split], train_input) * input_scale for rows in (own, foreign)]
    parts += [cross_dot(rows[:, split:], train_grad) * grad_scale for rows in (own, foreign)]
    pieces = jnp.stack(jnp.split(jnp.concatenate(parts), CORE, axis=1))
    lower, upper = exchange(pieces, "core").reshape(CORE, 2, CLASSES, -1, pieces.shape[2])
    upper = jnp.concatenate([upper[:, :2], upper[:, 3:], upper[:, 2:3]], axis=1)
    coded = encode(lower + upper)
    input_kernel, grad_kernel = decode(exchange(coded, "yl"), 2)
    product = (input_kernel * grad_kernel).reshape(VAL_SEQS, -1, input_kernel.shape[1])
    sums = jnp.sum(product, axis=(1, 2)) * (1.0 / SEQ_LEN)
    lanes = jnp.pad(sums, (0, LANES - VAL_SEQS))[None]
    column = exchange(jnp.broadcast_to(lanes, mine.shape), ("yh",) + TENSOR)
    first = jnp.sum(column * mine, axis=0, keepdims=True)
    total = first + jnp.sum(column * (1.0 - mine), axis=0, keepdims=True)
    planes = exchange(jnp.broadcast_to(total, (Z * X, LANES)), ("z", "x"))
    weight = jnp.sum(planes, axis=0, keepdims=True)
    return (first[:, :VAL_SEQS], jnp.sum(first * weight, axis=1))


def solution(mesh):
    fine = Mesh(mesh.devices.reshape(SIZES), DP + TENSOR)
    return jax.shard_map(
        per_device,
        mesh=fine,
        in_specs=(P(DP, TENSOR),) * 6,
        out_specs=(P(DP, None), P(DP)),
        check_vma=False,
    )
```

```python
import math

import jax
import jax.numpy as jnp
from jax import lax
from jax.experimental import pallas as pl
from jax.sharding import Mesh, PartitionSpec as P

D = 5120
FF = 20480
SEQ_LEN = 256
VAL_SEQS = 2
DP = ("yh", "z", "x")
TENSOR = ("yl", "core")
YH, Z, X, YL, CORE = SIZES = (2, 8, 4, 4, 2)
CLASSES = 4
LANES = 128
TAIL = 8
LOW, HIGH = -126.0, 30.0

inv_root_two = 0.7071067811865476
inv_root_tau = 0.3989422804014327


def output_grad(preact, upstream):
    preact_f = preact.astype(jnp.float32)
    derivative = (
        0.5 * (1.0 + lax.erf(preact_f * inv_root_two))
        + preact_f * jnp.exp(-0.5 * preact_f * preact_f) * inv_root_tau
    )
    return (upstream.astype(jnp.float32) * derivative).astype(jnp.bfloat16)


def cross_dot(left, right):
    return lax.dot_general(
        left, right, (((1,), (1,)), ((), ())), preferred_element_type=jnp.float32
    )


def exchange(value, axes, groups=None):
    return lax.all_to_all(value, axes, 0, 0, axis_index_groups=groups, tiled=True)


def place(yh, z, x):
    return (yh * Z + z % Z) * X + x % X


def class_groups():
    return [
        [place(yh, z, kind - 2 * z) for yh in range(YH) for z in range(Z)]
        for kind in range(CLASSES)
    ]


def device(yh, z, x, yl, core):
    return (place(yh, z, x) * YL + yl) * CORE + core


def shift(value, dz, dx):
    pairs = [
        (device(yh, z, x, yl, core), device(yh, z + turn * dz, x + turn * dx, yl, core))
        for yh in range(YH)
        for z in range(Z)
        for x in range(X)
        for yl in range(YL)
        for core, turn in enumerate((1, -1))
    ]
    return lax.ppermute(value, DP + TENSOR, pairs)


def valid_copies_kernel(input_ref, preact_ref, upstream_ref, out_ref, mine_ref):
    tensor = YL * CORE
    member = lax.broadcasted_iota(jnp.int32, mine_ref.shape, 0)
    mine_ref[...] = (member // tensor == lax.axis_index("yh")).astype(jnp.float32)
    split = input_ref.shape[1]
    joined = output_grad(preact_ref[...], upstream_ref[...])
    for member in range(out_ref.shape[0]):
        out_ref[member, :, :split] = input_ref[...]
        out_ref[member, :, split:] = joined


def class_gather(valid_input, valid_preact, valid_upstream):
    rows, split = valid_input.shape
    width = split + valid_preact.shape[1]
    members = YH * Z
    copies, mine = pl.pallas_call(
        valid_copies_kernel,
        out_shape=(
            jax.ShapeDtypeStruct((members, rows, width), jnp.bfloat16),
            jax.ShapeDtypeStruct((YH * YL * CORE, LANES), jnp.float32),
        ),
    )(valid_input, valid_preact, valid_upstream)
    return exchange(copies.reshape(members * rows, width), DP, class_groups()), mine


def neighbour_rows(own):
    first, second = shift(own, 0, 1), shift(own, 0, -1)
    across = shift(own, 1, 0)
    return jnp.concatenate([across, first, second])


def encode(parts):
    kinds, blocks, rows, lanes = parts.shape
    largest = jnp.max(jnp.abs(parts), axis=2)
    exponents = jnp.clip(jnp.ceil(jnp.log2(jnp.maximum(largest, 2.0**LOW))), LOW, HIGH)
    scale = jnp.exp2(-exponents)[:, :, None]
    scaled = [(parts[kind] * scale[kind]).astype(jnp.float16) for kind in range(kinds)]
    tail = jnp.pad(exponents.transpose(1, 0, 2), ((0, 0), (0, TAIL - kinds), (0, 0)))
    return jnp.concatenate(scaled + [tail.astype(jnp.float16)], axis=1)


def decode(coded, kinds):
    count, rows, lanes = coded.shape
    rows -= TAIL
    scale = jnp.exp2(coded[:, rows : rows + kinds].astype(jnp.float32))
    values = coded[:, :rows].astype(jnp.float32).reshape(count, kinds, rows // kinds, lanes)
    return jnp.sum(values * scale[:, :, None], axis=0)


def per_device(
    train_input, train_preact, train_upstream, valid_input, valid_preact, valid_upstream
):
    own, mine = class_gather(valid_input, valid_preact, valid_upstream)
    own, train_preact, train_upstream = lax.optimization_barrier(
        (own, train_preact, train_upstream)
    )
    foreign = neighbour_rows(own)
    train_grad = lax.optimization_barrier(output_grad(train_preact, train_upstream))
    split = valid_input.shape[1]
    input_scale, grad_scale = 1.0 / math.sqrt(D), 1.0 / math.sqrt(FF)
    parts = [cross_dot(rows[:, :split], train_input) * input_scale for rows in (own, foreign)]
    parts += [cross_dot(rows[:, split:], train_grad) * grad_scale for rows in (own, foreign)]
    pieces = jnp.stack(jnp.split(jnp.concatenate(parts), CORE, axis=1))
    lower, upper = exchange(pieces, "core").reshape(CORE, 2, CLASSES, -1, pieces.shape[2])
    upper = jnp.concatenate([upper[:, :2], upper[:, 3:], upper[:, 2:3]], axis=1)
    coded = encode(lower + upper)
    input_kernel, grad_kernel = decode(exchange(coded, "yl"), 2)
    product = (input_kernel * grad_kernel).reshape(VAL_SEQS, -1, input_kernel.shape[1])
    sums = jnp.sum(product, axis=(1, 2)) * (1.0 / SEQ_LEN)
    lanes = jnp.pad(sums, (0, LANES - VAL_SEQS))[None]
    column = exchange(jnp.broadcast_to(lanes, mine.shape), ("yh",) + TENSOR)
    first = jnp.sum(column * mine, axis=0, keepdims=True)
    total = first + jnp.sum(column * (1.0 - mine), axis=0, keepdims=True)
    planes = exchange(jnp.broadcast_to(total, (Z * X, LANES)), ("z", "x"))
    weight = jnp.sum(planes, axis=0, keepdims=True)
    return (first[:, :VAL_SEQS], jnp.sum(first * weight, axis=1))


def solution(mesh):
    fine = Mesh(mesh.devices.reshape(SIZES), DP + TENSOR)
    return jax.shard_map(
        per_device,
        mesh=fine,
        in_specs=(P(DP, TENSOR),) * 6,
        out_specs=(P(DP, None), P(DP)),
        check_vma=False,
    )
```

```python
import math

import jax
import jax.numpy as jnp
from jax import lax
from jax.experimental import pallas as pl
from jax.sharding import Mesh, PartitionSpec as P

D = 5120
FF = 20480
SEQ_LEN = 256
VAL_SEQS = 2
DP = ("yh", "z", "x")
TENSOR = ("yl", "core")
YH, Z, X, YL, CORE = SIZES = (2, 8, 4, 4, 2)
CLASSES = 4
LANES = 128
TAIL = 8
LOW, HIGH, TOP = -110.0, 30.0, 15.0

inv_root_two = 0.7071067811865476
inv_root_tau = 0.3989422804014327


def output_grad(preact, upstream):
    preact_f = preact.astype(jnp.float32)
    derivative = (
        0.5 * (1.0 + lax.erf(preact_f * inv_root_two))
        + preact_f * jnp.exp(-0.5 * preact_f * preact_f) * inv_root_tau
    )
    return (upstream.astype(jnp.float32) * derivative).astype(jnp.bfloat16)


def cross_dot(left, right):
    return lax.dot_general(
        left, right, (((1,), (1,)), ((), ())), preferred_element_type=jnp.float32
    )


def exchange(value, axes, groups=None):
    return lax.all_to_all(value, axes, 0, 0, axis_index_groups=groups, tiled=True)


def place(yh, z, x):
    return (yh * Z + z % Z) * X + x % X


def class_groups():
    return [
        [place(yh, z, kind - 2 * z) for yh in range(YH) for z in range(Z)]
        for kind in range(CLASSES)
    ]


def device(yh, z, x, yl, core):
    return (place(yh, z, x) * YL + yl) * CORE + core


def shift(value, dz, dx):
    pairs = [
        (device(yh, z, x, yl, core), device(yh, z + turn * dz, x + turn * dx, yl, core))
        for yh in range(YH)
        for z in range(Z)
        for x in range(X)
        for yl in range(YL)
        for core, turn in enumerate((1, -1))
    ]
    return lax.ppermute(value, DP + TENSOR, pairs)


def valid_rows_kernel(input_ref, preact_ref, upstream_ref, out_ref, mine_ref):
    member = lax.broadcasted_iota(jnp.int32, mine_ref.shape, 0)
    mine_ref[...] = (member // (YL * CORE) == lax.axis_index("yh")).astype(jnp.float32)
    split = input_ref.shape[1]
    out_ref[:, :split] = input_ref[...]
    out_ref[:, split:] = output_grad(preact_ref[...], upstream_ref[...])


def class_gather(valid_input, valid_preact, valid_upstream):
    rows, split = valid_input.shape
    width = split + valid_preact.shape[1]
    members = YH * Z
    valid, mine = pl.pallas_call(
        valid_rows_kernel,
        out_shape=(
            jax.ShapeDtypeStruct((rows, width), jnp.bfloat16),
            jax.ShapeDtypeStruct((YH * YL * CORE, LANES), jnp.float32),
        ),
    )(valid_input, valid_preact, valid_upstream)
    copies = jnp.broadcast_to(valid[None], (members, rows, width)).reshape(members * rows, width)
    return exchange(copies, DP, class_groups()), mine


def neighbour_rows(own):
    half = own.shape[0] // 2
    first, second = shift(own, 0, 1), shift(own, 0, -1)
    across = [shift(own[:half], 1, 0), shift(own[half:], -1, 0)]
    return jnp.concatenate(across + [first, second])


def encode(parts):
    kinds, blocks, rows, lanes = parts.shape
    largest = jnp.max(jnp.abs(parts), axis=2)
    exponents = jnp.clip(jnp.ceil(jnp.log2(jnp.maximum(largest, 2.0**LOW))), LOW, HIGH) - TOP
    scale = jnp.exp2(-exponents)[:, :, None]
    scaled = [(parts[kind] * scale[kind]).astype(jnp.float16) for kind in range(kinds)]
    tail = jnp.pad(exponents.transpose(1, 0, 2), ((0, 0), (0, TAIL - kinds), (0, 0)))
    return jnp.concatenate(scaled + [tail.astype(jnp.float16)], axis=1)


def decode(coded, kinds):
    count, rows, lanes = coded.shape
    rows -= TAIL
    scale = jnp.exp2(coded[:, rows : rows + kinds].astype(jnp.float32))
    values = coded[:, :rows].astype(jnp.float32).reshape(count, kinds, rows // kinds, lanes)
    return jnp.sum(values * scale[:, :, None], axis=0)


def per_device(
    train_input, train_preact, train_upstream, valid_input, valid_preact, valid_upstream
):
    own, mine = class_gather(valid_input, valid_preact, valid_upstream)
    own, train_preact, train_upstream = lax.optimization_barrier(
        (own, train_preact, train_upstream)
    )
    foreign = neighbour_rows(own)
    train_grad = lax.optimization_barrier(output_grad(train_preact, train_upstream))
    split = valid_input.shape[1]
    input_scale, grad_scale = 1.0 / math.sqrt(D), 1.0 / math.sqrt(FF)
    parts = [cross_dot(rows[:, :split], train_input) * input_scale for rows in (own, foreign)]
    parts += [cross_dot(rows[:, split:], train_grad) * grad_scale for rows in (own, foreign)]
    pieces = jnp.stack(jnp.split(jnp.concatenate(parts), CORE, axis=1))
    lower, upper = exchange(pieces, "core").reshape(CORE, 2, CLASSES, -1, pieces.shape[2])
    upper = jnp.concatenate([upper[:, :2], upper[:, 3:], upper[:, 2:3]], axis=1)
    coded = encode(lower + upper)
    input_kernel, grad_kernel = decode(exchange(coded, "yl"), 2)
    product = (input_kernel * grad_kernel).reshape(VAL_SEQS, -1, input_kernel.shape[1])
    sums = jnp.sum(product, axis=(1, 2)) * (1.0 / SEQ_LEN)
    lanes = jnp.pad(sums, (0, LANES - VAL_SEQS))[None]
    column = exchange(jnp.broadcast_to(lanes, mine.shape), ("yh",) + TENSOR)
    first = jnp.sum(column * mine, axis=0, keepdims=True)
    total = first + jnp.sum(column * (1.0 - mine), axis=0, keepdims=True)
    planes = exchange(jnp.broadcast_to(total, (Z * X, LANES)), ("z", "x"))
    weight = jnp.sum(planes, axis=0, keepdims=True)
    return (first[:, :VAL_SEQS], jnp.sum(first * weight, axis=1))


def solution(mesh):
    fine = Mesh(mesh.devices.reshape(SIZES), DP + TENSOR)
    return jax.shard_map(
        per_device,
        mesh=fine,
        in_specs=(P(DP, TENSOR),) * 6,
        out_specs=(P(DP, None), P(DP)),
        check_vma=False,
    )
```

```python
import math

import jax
import jax.numpy as jnp
from jax import lax
from jax.experimental import pallas as pl
from jax.sharding import Mesh, PartitionSpec as P

D = 5120
FF = 20480
SEQ_LEN = 256
VAL_SEQS = 2
DP = ("yh", "z", "x")
TENSOR = ("yl", "core")
YH, Z, X, YL, CORE = SIZES = (2, 8, 4, 4, 2)
CLASSES = 4
LANES = 128
TAIL = 8
LOW, HIGH, TOP = -110.0, 30.0, 15.0

inv_root_two = 0.7071067811865476
inv_root_tau = 0.3989422804014327


def output_grad(preact, upstream):
    preact_f = preact.astype(jnp.float32)
    derivative = (
        0.5 * (1.0 + lax.erf(preact_f * inv_root_two))
        + preact_f * jnp.exp(-0.5 * preact_f * preact_f) * inv_root_tau
    )
    return (upstream.astype(jnp.float32) * derivative).astype(jnp.bfloat16)


def cross_dot(left, right):
    return lax.dot_general(
        left, right, (((1,), (1,)), ((), ())), preferred_element_type=jnp.float32
    )


def exchange(value, axes, groups=None):
    return lax.all_to_all(value, axes, 0, 0, axis_index_groups=groups, tiled=True)


def place(yh, z, x):
    return (yh * Z + z % Z) * X + x % X


def class_groups():
    return [
        [place(yh, z, kind - 2 * z) for yh in range(YH) for z in range(Z)]
        for kind in range(CLASSES)
    ]


def device(yh, z, x, yl, core):
    return (place(yh, z, x) * YL + yl) * CORE + core


def shift(value, dz, dx):
    pairs = [
        (device(yh, z, x, yl, core), device(yh, z + turn * dz, x + turn * dx, yl, core))
        for yh in range(YH)
        for z in range(Z)
        for x in range(X)
        for yl in range(YL)
        for core, turn in enumerate((1, -1))
    ]
    return lax.ppermute(value, DP + TENSOR, pairs)


def valid_copies_kernel(input_ref, preact_ref, upstream_ref, out_ref, mine_ref, *core_refs):
    for core, core_ref in enumerate(core_refs):
        here = lax.axis_index("core") == core
        core_ref[...] = jnp.full(core_ref.shape, jnp.where(here, 1.0, 0.0), jnp.float32)
    tensor = YL * CORE
    member = lax.broadcasted_iota(jnp.int32, mine_ref.shape, 0)
    mine_ref[...] = (member // tensor == lax.axis_index("yh")).astype(jnp.float32)
    split = input_ref.shape[1]
    joined = output_grad(preact_ref[...], upstream_ref[...])
    for member in range(out_ref.shape[0]):
        out_ref[member, :, :split] = input_ref[...]
        out_ref[member, :, split:] = joined


def class_gather(valid_input, valid_preact, valid_upstream):
    rows, split = valid_input.shape
    width = split + valid_preact.shape[1]
    members = YH * Z
    copies, mine, *cores = pl.pallas_call(
        valid_copies_kernel,
        out_shape=(
            jax.ShapeDtypeStruct((members, rows, width), jnp.bfloat16),
            jax.ShapeDtypeStruct((YH * YL * CORE, LANES), jnp.float32),
        )
        + (jax.ShapeDtypeStruct((1, LANES), jnp.float32),) * CORE,
    )(valid_input, valid_preact, valid_upstream)
    return exchange(copies.reshape(members * rows, width), DP, class_groups()), mine, cores


def neighbour_rows(own):
    half = own.shape[0] // 2
    first, second = shift(own, 0, 1), shift(own, 0, -1)
    across = [shift(own[:half], 1, 0), shift(own[half:], -1, 0)]
    return jnp.concatenate(across + [first, second])


def encode(parts):
    kinds, blocks, rows, lanes = parts.shape
    largest = jnp.max(jnp.abs(parts), axis=2)
    exponents = jnp.clip(jnp.ceil(jnp.log2(jnp.maximum(largest, 2.0**LOW))), LOW, HIGH) - TOP
    scale = jnp.exp2(-exponents)[:, :, None]
    scaled = [(parts[kind] * scale[kind]).astype(jnp.float16) for kind in range(kinds)]
    tail = jnp.pad(exponents.transpose(1, 0, 2), ((0, 0), (0, TAIL - kinds), (0, 0)))
    return jnp.concatenate(scaled + [tail.astype(jnp.float16)], axis=1)


def decode(coded, kinds):
    count, rows, lanes = coded.shape
    rows -= TAIL
    scale = jnp.exp2(coded[:, rows : rows + kinds].astype(jnp.float32))
    values = coded[:, :rows].astype(jnp.float32).reshape(count, kinds, rows // kinds, lanes)
    return jnp.sum(values * scale[:, :, None], axis=0)


def per_device(
    train_input, train_preact, train_upstream, valid_input, valid_preact, valid_upstream
):
    own, mine, (is_first, is_second) = class_gather(valid_input, valid_preact, valid_upstream)
    own, train_preact, train_upstream = lax.optimization_barrier(
        (own, train_preact, train_upstream)
    )
    foreign = neighbour_rows(own)
    train_grad = lax.optimization_barrier(output_grad(train_preact, train_upstream))
    split = valid_input.shape[1]
    input_scale, grad_scale = 1.0 / math.sqrt(D), 1.0 / math.sqrt(FF)
    parts = [cross_dot(rows[:, :split], train_input) * input_scale for rows in (own, foreign)]
    parts += [cross_dot(rows[:, split:], train_grad) * grad_scale for rows in (own, foreign)]
    parts = jnp.concatenate(parts)
    lower, upper = parts[:, :LANES], parts[:, LANES:]
    sent = lower * is_second + upper * is_first
    kept = lower * is_first + upper * is_second
    other = lax.ppermute(sent, "core", [(0, 1), (1, 0)]).reshape(2, CLASSES, -1, LANES)
    other = jnp.concatenate([other[:, :2], other[:, 3:], other[:, 2:3]], axis=1)
    parts = kept.reshape(other.shape) + other
    coded = encode(parts)
    input_kernel, grad_kernel = decode(exchange(coded, "yl"), 2)
    product = (input_kernel * grad_kernel).reshape(VAL_SEQS, -1, input_kernel.shape[1])
    sums = jnp.sum(product, axis=(1, 2)) * (1.0 / SEQ_LEN)
    lanes = jnp.pad(sums, (0, LANES - VAL_SEQS))[None]
    column = exchange(jnp.broadcast_to(lanes, mine.shape), ("yh",) + TENSOR)
    first = jnp.sum(column * mine, axis=0, keepdims=True)
    total = first + jnp.sum(column * (1.0 - mine), axis=0, keepdims=True)
    planes = exchange(jnp.broadcast_to(total, (Z * X, LANES)), ("z", "x"))
    weight = jnp.sum(planes, axis=0, keepdims=True)
    return (first[:, :VAL_SEQS], jnp.sum(first * weight, axis=1))


def solution(mesh):
    fine = Mesh(mesh.devices.reshape(SIZES), DP + TENSOR)
    return jax.shard_map(
        per_device,
        mesh=fine,
        in_specs=(P(DP, TENSOR),) * 6,
        out_specs=(P(DP, None), P(DP)),
        check_vma=False,
    )
```

```python
import math

import jax
import jax.numpy as jnp
from jax import lax
from jax.experimental import pallas as pl
from jax.sharding import Mesh, PartitionSpec as P

D = 5120
FF = 20480
SEQ_LEN = 256
VAL_SEQS = 2
DP = ("yh", "z", "x")
TENSOR = ("yl", "core")
YH, Z, X, YL, CORE = SIZES = (2, 8, 4, 4, 2)
CLASSES = 4
LANES = 128
TAIL = 8
LOW, HIGH, TOP = -110.0, 30.0, 15.0

inv_root_two = 0.7071067811865476
inv_root_tau = 0.3989422804014327


def output_grad(preact, upstream):
    preact_f = preact.astype(jnp.float32)
    derivative = (
        0.5 * (1.0 + lax.erf(preact_f * inv_root_two))
        + preact_f * jnp.exp(-0.5 * preact_f * preact_f) * inv_root_tau
    )
    return (upstream.astype(jnp.float32) * derivative).astype(jnp.bfloat16)


def cross_dot(left, right):
    return lax.dot_general(
        left, right, (((1,), (1,)), ((), ())), preferred_element_type=jnp.float32
    )


def exchange(value, axes, groups=None):
    return lax.all_to_all(value, axes, 0, 0, axis_index_groups=groups, tiled=True)


def place(yh, z, x):
    return (yh * Z + z % Z) * X + x % X


def class_groups():
    return [
        [place(yh, z, kind - 2 * z) for yh in range(YH) for z in range(Z)]
        for kind in range(CLASSES)
    ]


def device(yh, z, x, yl, core):
    return (place(yh, z, x) * YL + yl) * CORE + core


def shift(value, dz, dx):
    pairs = [
        (device(yh, z, x, yl, core), device(yh, z + turn * dz, x + turn * dx, yl, core))
        for yh in range(YH)
        for z in range(Z)
        for x in range(X)
        for yl in range(YL)
        for core, turn in enumerate((1, -1))
    ]
    return lax.ppermute(value, DP + TENSOR, pairs)


def valid_copies_kernel(input_ref, preact_ref, upstream_ref, out_ref, mine_ref):
    tensor = YL * CORE
    member = lax.broadcasted_iota(jnp.int32, mine_ref.shape, 0)
    mine_ref[...] = (member // tensor == lax.axis_index("yh")).astype(jnp.float32)
    split = input_ref.shape[1]
    joined = output_grad(preact_ref[...], upstream_ref[...])
    for member in range(out_ref.shape[0]):
        out_ref[member, :, :split] = input_ref[...]
        out_ref[member, :, split:] = joined


def class_gather(valid_input, valid_preact, valid_upstream):
    rows, split = valid_input.shape
    width = split + valid_preact.shape[1]
    members = YH * Z
    copies, mine = pl.pallas_call(
        valid_copies_kernel,
        out_shape=(
            jax.ShapeDtypeStruct((members, rows, width), jnp.bfloat16),
            jax.ShapeDtypeStruct((YH * YL * CORE, LANES), jnp.float32),
        ),
    )(valid_input, valid_preact, valid_upstream)
    return exchange(copies.reshape(members * rows, width), DP, class_groups()), mine


def neighbour_rows(own):
    half = own.shape[0] // 2
    first, second = shift(own, 0, 1), shift(own, 0, -1)
    across = [shift(own[:half], 1, 0), shift(own[half:], -1, 0)]
    return jnp.concatenate(across + [first, second])


def encode(parts):
    kinds, blocks, rows, lanes = parts.shape
    largest = jnp.max(jnp.abs(parts), axis=2)
    exponents = jnp.clip(jnp.ceil(jnp.log2(jnp.maximum(largest, 2.0**LOW))), LOW, HIGH) - TOP
    scale = jnp.exp2(-exponents)[:, :, None]
    scaled = [(parts[kind] * scale[kind]).astype(jnp.float16) for kind in range(kinds)]
    tail = jnp.pad(exponents.transpose(1, 0, 2), ((0, 0), (0, TAIL - kinds), (0, 0)))
    return jnp.concatenate(scaled + [tail.astype(jnp.float16)], axis=1)


def decode(coded, kinds):
    count, rows, lanes = coded.shape
    rows -= TAIL
    scale = jnp.exp2(coded[:, rows : rows + kinds].astype(jnp.float32))
    values = coded[:, :rows].astype(jnp.float32).reshape(count, kinds, rows // kinds, lanes)
    return jnp.sum(values * scale[:, :, None], axis=0)


def per_device(
    train_input, train_preact, train_upstream, valid_input, valid_preact, valid_upstream
):
    own, mine = class_gather(valid_input, valid_preact, valid_upstream)
    own, train_preact, train_upstream = lax.optimization_barrier(
        (own, train_preact, train_upstream)
    )
    foreign = neighbour_rows(own)
    train_grad = lax.optimization_barrier(output_grad(train_preact, train_upstream))
    split = valid_input.shape[1]
    input_scale, grad_scale = 1.0 / math.sqrt(D), 1.0 / math.sqrt(FF)
    parts = [cross_dot(rows[:, :split], train_input) * input_scale for rows in (own, foreign)]
    parts += [cross_dot(rows[:, split:], train_grad) * grad_scale for rows in (own, foreign)]
    halves = zip(*(jnp.split(part, CORE, axis=1) for part in parts))
    pieces = jnp.concatenate([half for pieces in halves for half in pieces])
    lower, upper = exchange(pieces, "core").reshape(CORE, 2, CLASSES, -1, pieces.shape[1])
    upper = jnp.concatenate([upper[:, :2], upper[:, 3:], upper[:, 2:3]], axis=1)
    coded = encode(lower + upper)
    input_kernel, grad_kernel = decode(exchange(coded, "yl"), 2)
    product = (input_kernel * grad_kernel).reshape(VAL_SEQS, -1, input_kernel.shape[1])
    sums = jnp.sum(product, axis=(1, 2)) * (1.0 / SEQ_LEN)
    lanes = jnp.pad(sums, (0, LANES - VAL_SEQS))[None]
    column = exchange(jnp.broadcast_to(lanes, mine.shape), ("yh",) + TENSOR)
    first = jnp.sum(column * mine, axis=0, keepdims=True)
    total = first + jnp.sum(column * (1.0 - mine), axis=0, keepdims=True)
    planes = exchange(jnp.broadcast_to(total, (Z * X, LANES)), ("z", "x"))
    weight = jnp.sum(planes, axis=0, keepdims=True)
    return (first[:, :VAL_SEQS], jnp.sum(first * weight, axis=1))


def solution(mesh):
    fine = Mesh(mesh.devices.reshape(SIZES), DP + TENSOR)
    return jax.shard_map(
        per_device,
        mesh=fine,
        in_specs=(P(DP, TENSOR),) * 6,
        out_specs=(P(DP, None), P(DP)),
        check_vma=False,
    )
```

```python
import math

import jax
import jax.numpy as jnp
from jax import lax
from jax.experimental import pallas as pl
from jax.sharding import Mesh, PartitionSpec as P

D = 5120
FF = 20480
SEQ_LEN = 256
VAL_SEQS = 2
DP = ("yh", "z", "x")
TENSOR = ("yl", "core")
YH, Z, X, YL, CORE = SIZES = (2, 8, 4, 4, 2)
CLASSES = 4
LANES = 128
TAIL = 8
LOW, HIGH, TOP = -110.0, 30.0, 15.0

inv_root_two = 0.7071067811865476
inv_root_tau = 0.3989422804014327


def output_grad(preact, upstream):
    preact_f = preact.astype(jnp.float32)
    derivative = (
        0.5 * (1.0 + lax.erf(preact_f * inv_root_two))
        + preact_f * jnp.exp(-0.5 * preact_f * preact_f) * inv_root_tau
    )
    return (upstream.astype(jnp.float32) * derivative).astype(jnp.bfloat16)


def cross_dot(left, right):
    return lax.dot_general(
        left, right, (((1,), (1,)), ((), ())), preferred_element_type=jnp.float32
    )


def exchange(value, axes, groups=None):
    return lax.all_to_all(value, axes, 0, 0, axis_index_groups=groups, tiled=True)


def place(yh, z, x):
    return (yh * Z + z % Z) * X + x % X


def class_groups():
    return [
        [place(yh, z, kind - 2 * z) for yh in range(YH) for z in range(Z)]
        for kind in range(CLASSES)
    ]


def device(yh, z, x, yl, core):
    return (place(yh, z, x) * YL + yl) * CORE + core


def shift(value, dz, dx):
    pairs = [
        (device(yh, z, x, yl, core), device(yh, z + turn * dz, x + turn * dx, yl, core))
        for yh in range(YH)
        for z in range(Z)
        for x in range(X)
        for yl in range(YL)
        for core, turn in enumerate((1, -1))
    ]
    return lax.ppermute(value, DP + TENSOR, pairs)


def valid_copies_kernel(input_ref, preact_ref, upstream_ref, out_ref, mine_ref):
    tensor = YL * CORE
    member = lax.broadcasted_iota(jnp.int32, mine_ref.shape, 0)
    mine_ref[...] = (member // tensor == lax.axis_index("yh")).astype(jnp.float32)
    split = input_ref.shape[1]
    joined = output_grad(preact_ref[...], upstream_ref[...])
    for member in range(out_ref.shape[0]):
        out_ref[member, :, :split] = input_ref[...]
        out_ref[member, :, split:] = joined


def class_gather(valid_input, valid_preact, valid_upstream):
    rows, split = valid_input.shape
    width = split + valid_preact.shape[1]
    members = YH * Z
    copies, mine = pl.pallas_call(
        valid_copies_kernel,
        out_shape=(
            jax.ShapeDtypeStruct((members, rows, width), jnp.bfloat16),
            jax.ShapeDtypeStruct((YH * YL * CORE, LANES), jnp.float32),
        ),
    )(valid_input, valid_preact, valid_upstream)
    return exchange(copies.reshape(members * rows, width), DP, class_groups()), mine


def neighbour_rows(own):
    half = own.shape[0] // 2
    first, second = shift(own, 0, 1), shift(own, 0, -1)
    across = [shift(own[:half], 1, 0), shift(own[half:], -1, 0)]
    return jnp.concatenate(across), jnp.concatenate([first, second])


def encode(parts):
    kinds, blocks, rows, lanes = parts.shape
    largest = jnp.max(jnp.abs(parts), axis=2)
    exponents = jnp.clip(jnp.ceil(jnp.log2(jnp.maximum(largest, 2.0**LOW))), LOW, HIGH) - TOP
    scale = jnp.exp2(-exponents)[:, :, None]
    scaled = [(parts[kind] * scale[kind]).astype(jnp.float16) for kind in range(kinds)]
    tail = jnp.pad(exponents.transpose(1, 0, 2), ((0, 0), (0, TAIL - kinds), (0, 0)))
    return jnp.concatenate(scaled + [tail.astype(jnp.float16)], axis=1)


def decode(coded, kinds):
    count, rows, lanes = coded.shape
    rows -= TAIL
    scale = jnp.exp2(coded[:, rows : rows + kinds].astype(jnp.float32))
    values = coded[:, :rows].astype(jnp.float32).reshape(count, kinds, rows // kinds, lanes)
    return jnp.sum(values * scale[:, :, None], axis=0)


def per_device(
    train_input, train_preact, train_upstream, valid_input, valid_preact, valid_upstream
):
    own, mine = class_gather(valid_input, valid_preact, valid_upstream)
    own, train_preact, train_upstream = lax.optimization_barrier(
        (own, train_preact, train_upstream)
    )
    blocks = (own,) + neighbour_rows(own)
    train_grad = lax.optimization_barrier(output_grad(train_preact, train_upstream))
    split = valid_input.shape[1]
    input_scale, grad_scale = 1.0 / math.sqrt(D), 1.0 / math.sqrt(FF)
    parts = [cross_dot(rows[:, :split], train_input) * input_scale for rows in blocks]
    parts += [cross_dot(rows[:, split:], train_grad) * grad_scale for rows in blocks]
    halves = zip(*(jnp.split(part, CORE, axis=1) for part in parts))
    pieces = jnp.concatenate([half for pieces in halves for half in pieces])
    lower, upper = exchange(pieces, "core").reshape(CORE, 2, CLASSES, -1, pieces.shape[1])
    upper = jnp.concatenate([upper[:, :2], upper[:, 3:], upper[:, 2:3]], axis=1)
    coded = encode(lower + upper)
    input_kernel, grad_kernel = decode(exchange(coded, "yl"), 2)
    product = (input_kernel * grad_kernel).reshape(VAL_SEQS, -1, input_kernel.shape[1])
    sums = jnp.sum(product, axis=(1, 2)) * (1.0 / SEQ_LEN)
    lanes = jnp.pad(sums, (0, LANES - VAL_SEQS))[None]
    column = exchange(jnp.broadcast_to(lanes, mine.shape), ("yh",) + TENSOR)
    first = jnp.sum(column * mine, axis=0, keepdims=True)
    total = first + jnp.sum(column * (1.0 - mine), axis=0, keepdims=True)
    planes = exchange(jnp.broadcast_to(total, (Z * X, LANES)), ("z", "x"))
    weight = jnp.sum(planes, axis=0, keepdims=True)
    return (first[:, :VAL_SEQS], jnp.sum(first * weight, axis=1))


def solution(mesh):
    fine = Mesh(mesh.devices.reshape(SIZES), DP + TENSOR)
    return jax.shard_map(
        per_device,
        mesh=fine,
        in_specs=(P(DP, TENSOR),) * 6,
        out_specs=(P(DP, None), P(DP)),
        check_vma=False,
    )
```

```python
import math

import jax
import jax.numpy as jnp
from jax import lax
from jax.experimental import pallas as pl
from jax.sharding import Mesh, PartitionSpec as P

D = 5120
FF = 20480
SEQ_LEN = 256
VAL_SEQS = 2
DP = ("yh", "z", "x")
TENSOR = ("yl", "core")
YH, Z, X, YL, CORE = SIZES = (2, 8, 4, 4, 2)
CLASSES = 4
LANES = 128
TAIL = 8
LOW, HIGH, TOP = -110.0, 30.0, 15.0

inv_root_two = 0.7071067811865476
inv_root_tau = 0.3989422804014327


def output_grad(preact, upstream):
    preact_f = preact.astype(jnp.float32)
    derivative = (
        0.5 * (1.0 + lax.erf(preact_f * inv_root_two))
        + preact_f * jnp.exp(-0.5 * preact_f * preact_f) * inv_root_tau
    )
    return (upstream.astype(jnp.float32) * derivative).astype(jnp.bfloat16)


def cross_dot(left, right):
    return lax.dot_general(
        left, right, (((1,), (1,)), ((), ())), preferred_element_type=jnp.float32
    )


def exchange(value, axes, groups=None):
    return lax.all_to_all(value, axes, 0, 0, axis_index_groups=groups, tiled=True)


def place(yh, z, x):
    return (yh * Z + z % Z) * X + x % X


def class_groups():
    return [
        [
            place(yh, (kind - 2 * x) % 4 + 4 * far, x)
            for yh in range(YH)
            for x in range(X)
            for far in range(2)
        ]
        for kind in range(CLASSES)
    ]


def device(yh, z, x, yl, core):
    return (place(yh, z, x) * YL + yl) * CORE + core


def shift(value, dz, dx):
    pairs = [
        (device(yh, z, x, yl, core), device(yh, z + turn * dz, x + turn * dx, yl, core))
        for yh in range(YH)
        for z in range(Z)
        for x in range(X)
        for yl in range(YL)
        for core, turn in enumerate((1, -1))
    ]
    return lax.ppermute(value, DP + TENSOR, pairs)


def valid_copies_kernel(input_ref, preact_ref, upstream_ref, out_ref, mine_ref):
    tensor = YL * CORE
    member = lax.broadcasted_iota(jnp.int32, mine_ref.shape, 0)
    mine_ref[...] = (member // tensor == lax.axis_index("yh")).astype(jnp.float32)
    split = input_ref.shape[1]
    joined = output_grad(preact_ref[...], upstream_ref[...])
    for member in range(out_ref.shape[0]):
        out_ref[member, :, :split] = input_ref[...]
        out_ref[member, :, split:] = joined


def class_gather(valid_input, valid_preact, valid_upstream):
    rows, split = valid_input.shape
    width = split + valid_preact.shape[1]
    members = YH * Z
    copies, mine = pl.pallas_call(
        valid_copies_kernel,
        out_shape=(
            jax.ShapeDtypeStruct((members, rows, width), jnp.bfloat16),
            jax.ShapeDtypeStruct((YH * YL * CORE, LANES), jnp.float32),
        ),
    )(valid_input, valid_preact, valid_upstream)
    return exchange(copies.reshape(members * rows, width), DP, class_groups()), mine


def neighbour_rows(own):
    half = own.shape[0] // 2
    first, second = shift(own, 1, 0), shift(own, -1, 0)
    across = [shift(own[:half], 0, 1), shift(own[half:], 0, -1)]
    return jnp.concatenate(across + [first, second])


def encode(parts):
    kinds, blocks, rows, lanes = parts.shape
    largest = jnp.max(jnp.abs(parts), axis=2)
    exponents = jnp.clip(jnp.ceil(jnp.log2(jnp.maximum(largest, 2.0**LOW))), LOW, HIGH) - TOP
    scale = jnp.exp2(-exponents)[:, :, None]
    scaled = [(parts[kind] * scale[kind]).astype(jnp.float16) for kind in range(kinds)]
    tail = jnp.pad(exponents.transpose(1, 0, 2), ((0, 0), (0, TAIL - kinds), (0, 0)))
    return jnp.concatenate(scaled + [tail.astype(jnp.float16)], axis=1)


def decode(coded, kinds):
    count, rows, lanes = coded.shape
    rows -= TAIL
    scale = jnp.exp2(coded[:, rows : rows + kinds].astype(jnp.float32))
    values = coded[:, :rows].astype(jnp.float32).reshape(count, kinds, rows // kinds, lanes)
    return jnp.sum(values * scale[:, :, None], axis=0)


def per_device(
    train_input, train_preact, train_upstream, valid_input, valid_preact, valid_upstream
):
    own, mine = class_gather(valid_input, valid_preact, valid_upstream)
    own, train_preact, train_upstream = lax.optimization_barrier(
        (own, train_preact, train_upstream)
    )
    foreign = neighbour_rows(own)
    train_grad = lax.optimization_barrier(output_grad(train_preact, train_upstream))
    split = valid_input.shape[1]
    input_scale, grad_scale = 1.0 / math.sqrt(D), 1.0 / math.sqrt(FF)
    parts = [cross_dot(rows[:, :split], train_input) * input_scale for rows in (own, foreign)]
    parts += [cross_dot(rows[:, split:], train_grad) * grad_scale for rows in (own, foreign)]
    halves = zip(*(jnp.split(part, CORE, axis=1) for part in parts))
    pieces = jnp.concatenate([half for pieces in halves for half in pieces])
    lower, upper = exchange(pieces, "core").reshape(CORE, 2, CLASSES, -1, pieces.shape[1])
    upper = jnp.concatenate([upper[:, :2], upper[:, 3:], upper[:, 2:3]], axis=1)
    coded = encode(lower + upper)
    input_kernel, grad_kernel = decode(exchange(coded, "yl"), 2)
    product = (input_kernel * grad_kernel).reshape(VAL_SEQS, -1, input_kernel.shape[1])
    sums = jnp.sum(product, axis=(1, 2)) * (1.0 / SEQ_LEN)
    lanes = jnp.pad(sums, (0, LANES - VAL_SEQS))[None]
    column = exchange(jnp.broadcast_to(lanes, mine.shape), ("yh",) + TENSOR)
    first = jnp.sum(column * mine, axis=0, keepdims=True)
    total = first + jnp.sum(column * (1.0 - mine), axis=0, keepdims=True)
    planes = exchange(jnp.broadcast_to(total, (Z * X, LANES)), ("z", "x"))
    weight = jnp.sum(planes, axis=0, keepdims=True)
    return (first[:, :VAL_SEQS], jnp.sum(first * weight, axis=1))


def solution(mesh):
    fine = Mesh(mesh.devices.reshape(SIZES), DP + TENSOR)
    return jax.shard_map(
        per_device,
        mesh=fine,
        in_specs=(P(DP, TENSOR),) * 6,
        out_specs=(P(DP, None), P(DP)),
        check_vma=False,
    )
```
